32 devices in a mesh: group: 2 (over x), expert: 16 (over z, y, core).
Axes of the slice: x: 2, y: 2, z: 4, core: 2. Of those that a mesh axis runs over, the one named last changes fastest.
Arguments:
- tokens: bfloat16 [1536, 3584], P(('group', 'expert')), parts along dimension 0, may hold values from -6 to 6
- tangent: bfloat16 [1536, 3584], P(('group', 'expert')), parts along dimension 0, may hold values from -6 to 6
- routes: int32 [1536, 8], P(('group', 'expert')), parts along dimension 0, may hold values from 0 to 15, all different within a row; in each aligned block of 48 rows (0 to 47, 48 to 95, ...) at most 32 rows name the same one
- gates: float32 [1536, 8], P(('group', 'expert')), parts along dimension 0, may hold values from 0.1 to 1
- probes: float32 [1536, 16], P(('group', 'expert')), parts along dimension 0, may hold values from -0.21875 to 0.21875
- w_gate: bfloat16 [16, 3584, 1024], P('expert'), may hold values from -0.09375 to 0.09375
- w_up: bfloat16 [16, 3584, 1024], P('expert'), may hold values from -0.09375 to 0.09375
- w_down: bfloat16 [16, 1024, 3584], P('expert'), may hold values from -0.1875 to 0.1875
Outputs:
- curvature_rows: bfloat16 [1536, 3584], P(('group', 'expert')), parts along dimension 0
- sketch: float32 [32, 3584], P('group', 'expert'), parts along dimension 0
The draws below stay inside these ranges and needn't reach their ends.
There are 2 independent parts, one for each index of `group`. The reference program is written for one: setup_inputs(seed, part) draws one part's arguments, and reference() takes and returns one part's arrays. A program takes and returns all parts, laid end to end along the dimension named above; an argument that names none is the same for every part. Nothing has to cross between parts.
Inputs may be any that keep to these rules, and one draw needn't show every extreme that they name: `routes`: within one row the 8 experts differ. In each aligned block of 48 rows (the rows of one device) no expert is named by more than 32 rows, a bound that some block reaches.
All inputs are finite; a program needn't handle non-finite values.
Results may differ from the reference program's by a relative error of at most 0.0075.
Values may be sent and summed in bfloat16 or wider, within the bound.
No kernel may reach another device: no remote copies, remote signals or barrier semaphores. Data moves between devices by JAX's collectives and lax.ppermute only.
A program may use at most 128 MiB of HBM per device.

```python
import math
import jax
import jax.numpy as jnp
import numpy as np
from jax import lax

D = 3584
FFH = 1024
TOPK = 8
RANK = 16
TOK_DEV = 48
EXPERTS = 16
TOKENS = 768
CAP = 32
N_EXPERT = 16


def shard_levels(own_key, shape, shards, smallest, largest):
    loudness, own = 1.0, jax.random.fold_in(own_key, 6)
    for position, blocks in shards:
        steps = jnp.exp(jax.random.uniform(jax.random.fold_in(own, position), (blocks,), jnp.float32, smallest / len(shards), largest / len(shards)))
        loudness = loudness * jnp.repeat(steps, shape[position] // blocks).reshape([-1 if axis == position else 1 for axis in range(len(shape))])
    return loudness


def routed_block(key, own, number, rows, count, top, most, slope):
    ranking = jax.random.permutation(key, count)
    heavy_load, ordinary = load_shares(count, rows * top, most, slope, True), load_shares(count, rows * top, most, slope, False)
    places = jnp.arange(count)

    def named(sizes, rotation):
        used = int((sizes > 0).sum())
        fixed = max(1, used // 4)
        shifted = fixed + (places - fixed + rotation * (used - fixed)) % max(1, count - fixed)
        return jnp.zeros((count,), jnp.int32).at[ranking[jnp.where(places < fixed, places, shifted)]].set(jnp.asarray(sizes, jnp.int32))

    sizes = jnp.where(number % 4 == 0, named(heavy_load, number // 4), named(ordinary, number - number // 4 - 1))
    mixed = jax.random.permutation(jax.random.fold_in(own, 3), count)
    source_of, sink = mixed[0:count // 2 * 2:2], mixed[1:count // 2 * 2:2]
    room = jnp.minimum(sizes[source_of] - 1, most - sizes[sink]) // 2
    room = jnp.where((source_of == ranking[0]) | (sink == ranking[0]) | (sizes[sink] == 0), 0, jnp.maximum(room, 0))
    shifted = jax.random.randint(jax.random.fold_in(own, 4), (count // 2,), 0, 1 << 20) % (room + 1)
    sizes = sizes.at[source_of].add(-shifted).at[sink].add(shifted)
    labels = jnp.searchsorted(jnp.cumsum(sizes), jnp.arange(rows * top), side="right").astype(jnp.int32)
    listing = labels.reshape(top, rows).T
    listing = listing[jax.random.permutation(jax.random.fold_in(own, 1), rows)]
    rotation = jax.random.randint(jax.random.fold_in(own, 2), (rows, 1), 0, top)
    return jnp.take_along_axis(listing, (jnp.arange(top)[None, :] + rotation) % top, axis=1)


def load_shares(amount, total, limit, lean, full):
    weights = [(1 << 20) // math.isqrt(rank ** lean) + 1 for rank in range(1, amount + 1)]
    largest = limit if full else min(limit, max(-(-total // amount), total * weights[0] // sum(weights)))
    least = 1 if total - largest >= amount - 1 else 0
    holding, surplus = [largest] + [least] * (amount - 1), total - largest - least * (amount - 1)
    while surplus > 0:
        candidates = [i for i in range(1, amount) if holding[i] < largest] or [i for i in range(1, amount) if holding[i] < limit]
        mass, left = sum([weights[i] for i in candidates]), surplus
        for i in candidates:
            addition = min(limit - holding[i], max(1, left * weights[i] // mass), surplus)
            holding[i] = holding[i] + addition
            surplus = surplus - addition
    return np.array(holding)


def noise(key, extent, scale, bound, split=(), kind=jnp.bfloat16):
    values = scale * jax.random.normal(key, extent, jnp.float32)
    if split:
        values = values * shard_levels(key, extent, split, -0.22, 0.18)
    return jnp.clip(values, -bound, bound).astype(kind)


def setup_inputs(seed: int = 0, part: int = 0) -> dict:
    keys = jax.random.split(jax.random.key(seed), 9)
    part_splits = jax.random.split(jax.random.fold_in(keys[8], part), 9)
    tokens = noise(part_splits[0], (TOKENS, D), 1.0, 6.0, ((0, 16),))
    tangent = noise(part_splits[1], (TOKENS, D), 1.0, 6.0, ((0, 16),))
    routes_keys = jax.random.split(jax.random.fold_in(part_splits[2], 1), TOKENS // TOK_DEV)
    routes_turns = jax.random.permutation(jax.random.fold_in(part_splits[2], 3), TOKENS // TOK_DEV)
    routes = jax.vmap(lambda own, number: routed_block(jax.random.fold_in(part_splits[2], 2), own, number, TOK_DEV, EXPERTS, TOPK, CAP, 2))(routes_keys, routes_turns).reshape((TOKENS, TOPK))
    gates = jnp.clip(jnp.exp(math.log(1.0) - 2.3025851 * jax.random.uniform(part_splits[3], (TOKENS, TOPK), jnp.float32) ** shard_levels(part_splits[3], (TOKENS, TOPK), ((0, 16),), -0.2, 0.2)), 0.1, 1.0)
    probes = noise(part_splits[4], (TOKENS, RANK), TOKENS ** -0.5, 0.21875, ((0, 16),), jnp.float32)
    w_gate = noise(keys[5], (EXPERTS, D, FFH), D ** -0.5, 0.09375, ((0, 16),))
    w_up = noise(keys[6], (EXPERTS, D, FFH), D ** -0.5, 0.09375, ((0, 16),))
    w_down = noise(keys[7], (EXPERTS, FFH, D), FFH ** -0.5, 0.1875, ((0, 16),))
    return {"tokens": tokens, "tangent": tangent, "routes": routes, "gates": gates, "probes": probes, "w_gate": w_gate, "w_up": w_up, "w_down": w_down}


def dsilu(value):
    sig = jax.nn.sigmoid(value)
    return sig * (1.0 + value * (1.0 - sig))


def reference(tokens, tangent, routes, gates, probes, w_gate, w_up, w_down):
    flat = routes.reshape(-1).astype(jnp.int32)
    total = flat.shape[0]
    owner = jnp.arange(total, dtype=jnp.int32) // TOPK
    most = N_EXPERT * CAP
    expert_ids = jnp.arange(EXPERTS, dtype=jnp.int32)

    def locate(expert):
        where = jnp.nonzero(flat == expert, size=most, fill_value=total)[0].astype(jnp.int32)
        live = where < total
        token_ids = jnp.where(live, owner[jnp.minimum(where, total - 1)], 0).astype(jnp.int32)
        return where, live, token_ids

    def first(carry, inputs):
        expert, w_g, w_u, w_d = inputs
        where, live, token_ids = locate(expert)
        rows = jnp.where(live[:, None], tokens[token_ids], jnp.zeros((), jnp.bfloat16))
        tans = jnp.where(live[:, None], tangent[token_ids], jnp.zeros((), jnp.bfloat16))
        pre_a = jnp.dot(rows, w_g, preferred_element_type=jnp.float32)
        pre_b = jnp.dot(rows, w_u, preferred_element_type=jnp.float32)
        tan_a = jnp.dot(tans, w_g, preferred_element_type=jnp.float32)
        tan_b = jnp.dot(tans, w_u, preferred_element_type=jnp.float32)
        hidden = (dsilu(pre_a) * tan_a * pre_b + jax.nn.silu(pre_a) * tan_b).astype(jnp.bfloat16)
        tout = jnp.dot(hidden, w_d, preferred_element_type=jnp.float32).astype(jnp.bfloat16)
        carry = carry.at[where].set(tout)
        return carry, (pre_a, pre_b)

    start = jnp.zeros((total + 1, D), jnp.bfloat16)
    tout_all, saved = lax.scan(first, start, (expert_ids, w_gate, w_up, w_down))
    tout_rows = tout_all[:total].reshape(TOKENS, TOPK, D).astype(jnp.float32)
    ty = jnp.sum(gates[:, :, None] * tout_rows, axis=1).astype(jnp.bfloat16)

    def second(carry, inputs):
        expert, pre_a, pre_b, w_g, w_u, w_d = inputs
        where, live, token_ids = locate(expert)
        rows = jnp.where(live[:, None], ty[token_ids], jnp.zeros((), jnp.bfloat16))
        grad_h = lax.dot_general(rows, w_d, (((1,), (1,)), ((), ())), preferred_element_type=jnp.float32)
        grad_a = (grad_h * pre_b * dsilu(pre_a)).astype(jnp.bfloat16)
        grad_b = (grad_h * jax.nn.silu(pre_a)).astype(jnp.bfloat16)
        back = lax.dot_general(grad_a, w_g, (((1,), (1,)), ((), ())), preferred_element_type=jnp.float32)
        back = back + lax.dot_general(grad_b, w_u, (((1,), (1,)), ((), ())), preferred_element_type=jnp.float32)
        carry = carry.at[where].set(back.astype(jnp.bfloat16))
        return carry, None

    q_all, unused = lax.scan(second, start, (expert_ids, saved[0], saved[1], w_gate, w_up, w_down))
    q_rows = q_all[:total].reshape(TOKENS, TOPK, D).astype(jnp.float32)
    curvature_rows = jnp.sum(gates[:, :, None] * q_rows, axis=1).astype(jnp.bfloat16)
    sketch = lax.dot_general(probes, curvature_rows.astype(jnp.float32), (((0,), (0,)), ((), ())), precision=lax.Precision.HIGHEST, preferred_element_type=jnp.float32)
    return curvature_rows, sketch
```

```python
import functools

import jax
import jax.numpy as jnp
from jax import lax
from jax.experimental import pallas as pl
from jax.experimental.pallas import tpu as pltpu
from jax.sharding import PartitionSpec as P

BF16 = jnp.bfloat16
F32 = jnp.float32
VMEM_BYTES = 48 * 1024 * 1024


def swap(values, perm):
    return lax.ppermute(values, "expert", perm)


def mm(left, right):
    return jnp.dot(left, right, preferred_element_type=F32)


def mm_t(left, right):
    return lax.dot_general(left, right, (((1,), (1,)), ((), ())), preferred_element_type=F32)


def up_kernel(f_steps, rows, p0, p1, p2, p3, gate, w_g, w_u, w_d, keep, send, u_out, v_out, x_all, th_all, sems):
    step = pl.program_id(0)
    block = 4 * rows
    f_tile = w_g.shape[1]

    @pl.when(step == 0)
    def _():
        copies = []
        for j, piece in enumerate((p0, p1, p2, p3)):
            for part in range(2):
                copies.append(
                    pltpu.make_async_copy(
                        piece.at[pl.ds(part * rows, rows)],
                        x_all.at[pl.ds(part * block + j * rows, rows)],
                        sems.at[2 * j + part],
                    )
                )
        for copy in copies:
            copy.start()
        for copy in copies:
            copy.wait()

    @pl.when(step < f_steps)
    def _():
        x = x_all[...]
        both_a = mm(x, w_g[...])
        both_b = mm(x, w_u[...])
        a, ta = both_a[:block], both_a[block:]
        b, tb = both_b[:block], both_b[block:]
        sig = jax.nn.sigmoid(a)
        g = gate[...]
        u = (sig * (1.0 + a * (1.0 - sig))) * b * g
        v = a * sig * g
        u_out[...] = u
        v_out[...] = v
        th_all[step] = (u * ta + v * tb).astype(BF16)

    @pl.when(step >= f_steps)
    def _():
        out = mm(th_all[0], w_d[pl.ds(0, f_tile), :])
        for k in range(1, f_steps):
            out = out + mm(th_all[k], w_d[pl.ds(k * f_tile, f_tile), :])
        out = out.astype(BF16)
        keep[...] = out[: 2 * rows]
        send[...] = out[2 * rows :]


def down_kernel(f_steps, rows, p0, p1, p2, p3, u_in, v_in, w_d, w_g, w_u, keep, send, x_all, ga_all, gb_all, sems):
    step = pl.program_id(0)
    f_tile = w_d.shape[0]

    @pl.when(step == 0)
    def _():
        copies = []
        for j, piece in enumerate((p0, p1, p2, p3)):
            copies.append(pltpu.make_async_copy(piece, x_all.at[pl.ds(j * rows, rows)], sems.at[j]))
        for copy in copies:
            copy.start()
        for copy in copies:
            copy.wait()

    @pl.when(step < f_steps)
    def _():
        gh = mm_t(x_all[...], w_d[...])
        ga_all[step] = (gh * u_in[...]).astype(BF16)
        gb_all[step] = (gh * v_in[...]).astype(BF16)

    @pl.when(step >= f_steps)
    def _():
        out = None
        for k in range(f_steps):
            columns = pl.ds(k * f_tile, f_tile)
            term = mm_t(ga_all[k], w_g[:, columns]) + mm_t(gb_all[k], w_u[:, columns])
            out = term if out is None else out + term
        out = out.astype(BF16)
        keep[...] = out[: 2 * rows]
        send[...] = out[2 * rows :]


def tile_of(size, most):
    for tile in range(min(size, most), 0, -128):
        if size % tile == 0 and tile % 128 == 0:
            return tile
    return size


def up_call(pieces, gate, w_g, w_u, w_d):
    width, hidden = w_g.shape
    rows = pieces[0].shape[0] // 2
    f_tile, d_tile = tile_of(hidden, 256), tile_of(width, 896)
    f_steps, d_steps = hidden // f_tile, width // d_tile
    first = lambda i: jnp.minimum(i, f_steps - 1)
    second = lambda i: jnp.maximum(i - f_steps, 0)
    block = 4 * rows
    flops = 2 * width * hidden * block * 5
    return pl.pallas_call(
        functools.partial(up_kernel, f_steps, rows),
        grid=(f_steps + d_steps,),
        in_specs=[pl.BlockSpec(memory_space=pl.ANY)] * 4
        + [
            pl.BlockSpec((block, 1), lambda i: (0, 0)),
            pl.BlockSpec((width, f_tile), lambda i: (0, first(i))),
            pl.BlockSpec((width, f_tile), lambda i: (0, first(i))),
            pl.BlockSpec((hidden, d_tile), lambda i: (0, second(i))),
        ],
        out_specs=[
            pl.BlockSpec((2 * rows, d_tile), lambda i: (0, second(i))),
            pl.BlockSpec((2 * rows, d_tile), lambda i: (0, second(i))),
            pl.BlockSpec((block, f_tile), lambda i: (0, first(i))),
            pl.BlockSpec((block, f_tile), lambda i: (0, first(i))),
        ],
        out_shape=[
            jax.ShapeDtypeStruct((2 * rows, width), BF16),
            jax.ShapeDtypeStruct((2 * rows, width), BF16),
            jax.ShapeDtypeStruct((block, hidden), F32),
            jax.ShapeDtypeStruct((block, hidden), F32),
        ],
        scratch_shapes=[
            pltpu.VMEM((2 * block, width), BF16),
            pltpu.VMEM((f_steps, block, f_tile), BF16),
            pltpu.SemaphoreType.DMA((8,)),
        ],
        compiler_params=pltpu.CompilerParams(vmem_limit_bytes=VMEM_BYTES),
        cost_estimate=pl.CostEstimate(flops=flops, bytes_accessed=6 * width * hidden, transcendentals=0),
    )(*pieces, gate, w_g, w_u, w_d)


def down_call(pieces, u, v, w_g, w_u, w_d):
    width, hidden = w_g.shape
    rows = pieces[0].shape[0]
    f_tile, d_tile = tile_of(hidden, 256), tile_of(width, 896)
    f_steps, d_steps = hidden // f_tile, width // d_tile
    first = lambda i: jnp.minimum(i, f_steps - 1)
    second = lambda i: jnp.maximum(i - f_steps, 0)
    block = 4 * rows
    flops = 2 * width * hidden * block * 3
    return pl.pallas_call(
        functools.partial(down_kernel, f_steps, rows),
        grid=(f_steps + d_steps,),
        in_specs=[pl.BlockSpec(memory_space=pl.ANY)] * 4
        + [
            pl.BlockSpec((block, f_tile), lambda i: (0, first(i))),
            pl.BlockSpec((block, f_tile), lambda i: (0, first(i))),
            pl.BlockSpec((f_tile, width), lambda i: (first(i), 0)),
            pl.BlockSpec((d_tile, hidden), lambda i: (second(i), 0)),
            pl.BlockSpec((d_tile, hidden), lambda i: (second(i), 0)),
        ],
        out_specs=[
            pl.BlockSpec((2 * rows, d_tile), lambda i: (0, second(i))),
            pl.BlockSpec((2 * rows, d_tile), lambda i: (0, second(i))),
        ],
        out_shape=[
            jax.ShapeDtypeStruct((2 * rows, width), BF16),
            jax.ShapeDtypeStruct((2 * rows, width), BF16),
        ],
        scratch_shapes=[
            pltpu.VMEM((block, width), BF16),
            pltpu.VMEM((f_steps, block, f_tile), BF16),
            pltpu.VMEM((f_steps, block, f_tile), BF16),
            pltpu.SemaphoreType.DMA((4,)),
        ],
        compiler_params=pltpu.CompilerParams(vmem_limit_bytes=VMEM_BYTES),
        cost_estimate=pl.CostEstimate(flops=flops, bytes_accessed=6 * width * hidden, transcendentals=0),
    )(*pieces, u, v, w_d, w_g, w_u)


def gather_blocks(own, ring, across, pair):
    depth = len(ring) // 4
    blocks, held = [], own
    for s in range(depth):
        other = swap(held, across)
        blocks.append((held, other, swap(held, pair), swap(other, pair)))
        if s < depth - 1:
            held = swap(held, ring)
    return blocks


def scatter_sum(halves, ring, across, pair):
    depth = len(halves)
    rows = halves[0][0].shape[0] // 2
    moving = None
    for s in list(range(1, depth)) + [0]:
        keep, send = halves[s]
        got = swap(send, pair)
        far = (keep[rows:].astype(F32) + got[rows:].astype(F32)).astype(BF16)
        total = keep[:rows].astype(F32) + got[:rows].astype(F32) + swap(far, across).astype(F32)
        if moving is not None:
            total = total + moving.astype(F32)
        if s:
            moving = swap(total.astype(BF16), ring)
    return total.astype(BF16)


def body(tokens, tangent, routes, gates, probes, w_gate, w_up, w_down):
    rows, width = tokens.shape
    count = lax.axis_size("expert")
    depth = count // 4
    ring = [(i, (i + 4) % count) for i in range(count)]
    across = [(i, i ^ 2) for i in range(count)]
    pair = [(i, i ^ 1) for i in range(count)]
    w_g, w_u, w_d = w_gate[0], w_up[0], w_down[0]
    me = lax.axis_index("expert")

    experts = jnp.arange(count, dtype=jnp.int32)
    hit = routes[None, :, :] == experts[:, None, None]
    dense = jnp.sum(jnp.where(hit, gates[None], 0.0), axis=2)
    dense = lax.all_to_all(dense, "expert", split_axis=0, concat_axis=0, tiled=True)
    order = jnp.arange(count, dtype=jnp.int32)
    flip = jnp.array([0, 2, 1, 3], jnp.int32)[order % 4]
    source = ((me // 4 - order // 4 + depth) % depth) * 4 + ((me % 4) ^ flip)
    dense = jnp.take(dense, source, axis=0).reshape(depth, 4 * rows, 1)

    stacked = jnp.concatenate([tokens, tangent], axis=0)
    blocks = gather_blocks(stacked, ring, across, pair)
    halves, saved = [], []
    for s in range(depth):
        keep, send, u, v = up_call(blocks[s], dense[s], w_g, w_u, w_d)
        halves.append((keep, send))
        saved.append((u, v))
    combined = scatter_sum(halves, ring, across, pair)
    blocks = gather_blocks(combined, ring, across, pair)
    halves = [down_call(blocks[s], *saved[s], w_g, w_u, w_d) for s in range(depth)]
    curvature_rows = scatter_sum(halves, ring, across, pair)
    term = lax.dot_general(
        probes,
        curvature_rows.astype(F32),
        (((0,), (0,)), ((), ())),
        precision=lax.Precision.HIGHEST,
        preferred_element_type=F32,
    )
    share = width // count
    rank = term.shape[0]
    term = term.reshape(rank, count, share).transpose(1, 0, 2)
    term = lax.all_to_all(term, "expert", split_axis=0, concat_axis=0, tiled=True)
    sketch = jnp.sum(term, axis=0)
    return (curvature_rows, sketch)


def solution(mesh):
    return jax.shard_map(
        body,
        mesh=mesh,
        in_specs=(
            P(("group", "expert"), None),
            P(("group", "expert"), None),
            P(("group", "expert"), None),
            P(("group", "expert"), None),
            P(("group", "expert"), None),
            P("expert", None, None),
            P("expert", None, None),
            P("expert", None, None),
        ),
        out_specs=(P(("group", "expert"), None), P("group", "expert")),
        check_vma=False,
    )
```

```python
import functools

import jax
import jax.numpy as jnp
from jax import lax
from jax.experimental import pallas as pl
from jax.experimental.pallas import tpu as pltpu
from jax.sharding import PartitionSpec as P

BF16 = jnp.bfloat16
F32 = jnp.float32
UP_BYTES = 12 * 1024 * 1024
DOWN_BYTES = 12 * 1024 * 1024


def swap(values, perm):
    return lax.ppermute(values, "expert", perm)


def mm(left, right):
    return jnp.dot(left, right, preferred_element_type=F32)


def mm_t(left, right):
    return lax.dot_general(left, right, (((1,), (1,)), ((), ())), preferred_element_type=F32)


def tile_of(size, most):
    for tile in range(min(size, most), 0, -128):
        if size % tile == 0 and tile % 128 == 0:
            return tile
    return size


def load_all(copies):
    for copy in copies:
        copy.start()
    for copy in copies:
        copy.wait()


def up_kernel(f_tile, d_tile, count, *refs):
    pieces, refs = refs[:4], refs[4:]
    me, w_g, w_u, w_d, keep, send, u_out, v_out, probes_out, x_all, gates, probes, th_all, sems = refs
    width, hidden = w_g.shape
    rows = pieces[0].shape[0] // 2
    block = 4 * rows
    half = block // 2
    copies = []
    for j, piece in enumerate(pieces):
        for part in range(2):
            source = piece.at[pl.ds(part * rows, rows), pl.ds(0, width)]
            target = x_all.at[pl.ds(part * block + j * rows, rows)]
            copies.append(pltpu.make_async_copy(source, target, sems.at[4 * j + part]))
            source = piece.at[pl.ds(part * rows, rows), pl.ds(width, gates.shape[1])]
            target = (gates, probes)[part].at[pl.ds(j * rows, rows)]
            copies.append(pltpu.make_async_copy(source, target, sems.at[4 * j + 2 + part]))
    load_all(copies)
    lane = lax.broadcasted_iota(jnp.int32, gates.shape, 1) - me[0]
    hit = (lane == 0) | (lane == count) | (lane == 2 * count)
    g = jnp.sum(jnp.where(hit, gates[...].astype(F32), 0.0), axis=1, keepdims=True)
    probes_out[...] = probes[...].astype(F32).T.astype(BF16)

    def first(i, carry):
        cols = pl.ds(pl.multiple_of(i * f_tile, f_tile), f_tile)
        x = x_all[...]
        both_a = mm(x, w_g[:, cols])
        both_b = mm(x, w_u[:, cols])
        a, ta = both_a[:block], both_a[block:]
        b, tb = both_b[:block], both_b[block:]
        sig = jax.nn.sigmoid(a)
        u = (sig * (1.0 + a * (1.0 - sig))) * b * g
        v = a * sig * g
        u_out[:, cols] = u
        v_out[:, cols] = v
        th_all[:, cols] = (u * ta + v * tb).astype(BF16)
        return carry

    lax.fori_loop(0, hidden // f_tile, first, 0)

    def second(i, carry):
        cols = pl.ds(pl.multiple_of(i * d_tile, d_tile), d_tile)
        out = mm(th_all[...], w_d[:, cols]).astype(BF16)
        keep[:, cols] = out[:half]
        send[:, cols] = out[half:]
        return carry

    lax.fori_loop(0, width // d_tile, second, 0)


def down_kernel(f_tile, d_tile, rank, *refs):
    pieces, refs = refs[:4], refs[4:]
    u_in, v_in, probes, before, w_g, w_u, w_d, keep, send, term, x_all, ga, gb, sems = refs
    half = u_in.shape[0] // 2
    width, hidden = w_g.shape
    rows = pieces[0].shape[0]
    load_all(
        [
            pltpu.make_async_copy(piece, x_all.at[pl.ds(j * rows, rows)], sems.at[j])
            for j, piece in enumerate(pieces)
        ]
    )

    def first(i, carry):
        cols = pl.ds(pl.multiple_of(i * f_tile, f_tile), f_tile)
        gh = mm_t(x_all[...], w_d[cols, :])
        ga[:, cols] = (gh * u_in[:, cols]).astype(BF16)
        gb[:, cols] = (gh * v_in[:, cols]).astype(BF16)
        return carry

    lax.fori_loop(0, hidden // f_tile, first, 0)

    def second(i, carry):
        cols = pl.ds(pl.multiple_of(i * d_tile, d_tile), d_tile)
        out = (mm_t(ga[...], w_g[cols, :]) + mm_t(gb[...], w_u[cols, :])).astype(BF16)
        keep[:, cols] = out[:half]
        send[:, cols] = out[half:]
        parts = mm(probes[...], out)
        term[:, cols] = before[:, cols] + (parts[:rank] + parts[rank : 2 * rank] + parts[2 * rank : 3 * rank])
        return carry

    lax.fori_loop(0, width // d_tile, second, 0)


ANY = pl.BlockSpec(memory_space=pl.ANY)
WHOLE = pl.BlockSpec(memory_space=pltpu.VMEM)


def up_call(pieces, me, count, w_g, w_u, w_d):
    width, hidden = w_g.shape
    block, lanes = 2 * pieces[0].shape[0], pieces[0].shape[1] - width
    return pl.pallas_call(
        functools.partial(up_kernel, tile_of(hidden, 1024), tile_of(width, 3584), count),
        in_specs=[ANY] * 4 + [pl.BlockSpec(memory_space=pltpu.SMEM)] + [WHOLE] * 3,
        out_specs=[WHOLE] * 5,
        out_shape=[jax.ShapeDtypeStruct((block // 2, width), BF16)] * 2
        + [jax.ShapeDtypeStruct((block, hidden), F32)] * 2
        + [jax.ShapeDtypeStruct((lanes, block), BF16)],
        scratch_shapes=[
            pltpu.VMEM((2 * block, width), BF16),
            pltpu.VMEM((block, lanes), BF16),
            pltpu.VMEM((block, lanes), BF16),
            pltpu.VMEM((block, hidden), BF16),
            pltpu.SemaphoreType.DMA((16,)),
        ],
        compiler_params=pltpu.CompilerParams(vmem_limit_bytes=UP_BYTES),
        cost_estimate=pl.CostEstimate(flops=10 * width * hidden * block, bytes_accessed=2**20, transcendentals=0),
    )(*pieces, me, w_g, w_u, w_d)


def down_call(pieces, u, v, probes, before, w_g, w_u, w_d):
    width, hidden = w_g.shape
    rank = before.shape[0]
    block = u.shape[0]
    return pl.pallas_call(
        functools.partial(down_kernel, tile_of(hidden, 1024), tile_of(width, 3584), rank),
        in_specs=[ANY] * 4 + [WHOLE] * 7,
        out_specs=[WHOLE] * 3,
        out_shape=[jax.ShapeDtypeStruct((block // 2, width), BF16)] * 2 + [jax.ShapeDtypeStruct((rank, width), F32)],
        scratch_shapes=[
            pltpu.VMEM((block, width), BF16),
            pltpu.VMEM((block, hidden), BF16),
            pltpu.VMEM((block, hidden), BF16),
            pltpu.SemaphoreType.DMA((4,)),
        ],
        compiler_params=pltpu.CompilerParams(vmem_limit_bytes=DOWN_BYTES),
        cost_estimate=pl.CostEstimate(flops=6 * width * hidden * block, bytes_accessed=2**20, transcendentals=0),
    )(*pieces, u, v, probes, before, w_g, w_u, w_d)


def arrange_kernel(me, term, out):
    depth, share = out.shape[1], out.shape[3]
    plane, spot = me[0] // 4, me[0] % 4
    for d in range(4 * depth):
        back = lax.rem(plane + (depth - d // 4), depth)
        gap = spot ^ (d % 4)
        piece = (gap >> 1) | ((gap & 1) << 1)
        out[piece, back] = term[:, d * share : (d + 1) * share]


def arrange_call(term, me, count):
    rank, width = term.shape
    return pl.pallas_call(
        arrange_kernel,
        in_specs=[pl.BlockSpec(memory_space=pltpu.SMEM), WHOLE],
        out_specs=WHOLE,
        out_shape=jax.ShapeDtypeStruct((4, count // 4, rank, width // count), F32),
        compiler_params=pltpu.CompilerParams(vmem_limit_bytes=4 * 1024 * 1024),
    )(me, term)


def phase(own, split, compute, turns, side, ring, across, pair, depth):
    near, far, near_mate = [own], [], []
    pieces, made, extras, ready = {}, {}, {}, {}
    moving = None
    for turn in range(2 * depth):
        flight = {}
        if turn < depth:
            if turn < depth - 1:
                flight["near"] = swap(near[turn], ring)
                flight["far"] = swap(near[turn], across)
            elif split is None:
                flight["far"] = swap(near[turn], across)
            else:
                flight["far_low"] = swap(near[turn][:split], across)
                flight["far_high"] = swap(far[turn - 1][split:], ring)
            flight["near_mate"] = swap(near[turn], pair)
        if 0 <= turn - 1 < depth:
            back = turn - 1
            pieces[back] = (near[back], far[back], near_mate[back], swap(far[back], pair))
        if turn in turns:
            flight["made"] = compute(turns[turn], pieces.pop(turns[turn]))
        flight["pieces"] = dict(pieces)
        due = turn - depth + 1
        if due >= 1:
            due_base, crossing = ready.pop(due % depth)
            flight["cross"] = swap(crossing, across)
            if due > 1:
                flight["moving"] = swap(moving, ring)
        if turn - 1 in turns:
            keep, send = made[turns[turn - 1]]
            rows = keep.shape[0] // 2
            got = swap(send, pair)
            base = (keep[:rows].astype(F32) + got[:rows].astype(F32)).astype(BF16)
            outward = (keep[rows:].astype(F32) + got[rows:].astype(F32)).astype(BF16)
            flight["ready"] = (base, outward)
        if side is not None:
            flight["side"] = side[0](turn, extras)
        flight["waiting"] = dict(ready)
        names = list(flight)
        flight = dict(zip(names, lax.optimization_barrier([flight[name] for name in names])))
        if "near" in flight:
            near.append(flight["near"])
        if "far" in flight:
            far.append(flight["far"])
        if "far_low" in flight:
            far.append(jnp.concatenate([flight["far_low"], flight["far_high"]], axis=0))
        if "near_mate" in flight:
            near_mate.append(flight["near_mate"])
        pieces = flight["pieces"]
        if "made" in flight:
            made[turns[turn]] = flight["made"][:2]
            extras[turns[turn]] = flight["made"][2]
            if side is not None:
                side[1](turn, flight["made"][2])
        elif side is not None and turn > depth:
            side[1](turn, flight["side"])
        ready = flight["waiting"]
        if "ready" in flight:
            ready[turns[turn - 1]] = flight["ready"]
        if due >= 1:
            total = due_base.astype(F32) + flight["cross"].astype(F32)
            if "moving" in flight:
                total = total + flight["moving"].astype(F32)
            moving = total.astype(BF16)
    return moving, extras, flight.get("side")


def body(tokens, tangent, routes, gates, probes, w_gate, w_up, w_down):
    rows, width = tokens.shape
    count = lax.axis_size("expert")
    depth = count // 4
    ring = [(i, (i + 4) % count) for i in range(count)]
    across = [(i, i ^ 2) for i in range(count)]
    pair = [(i, i ^ 1) for i in range(count)]
    w_g, w_u, w_d = w_gate[0], w_up[0], w_down[0]
    me = lax.axis_index("expert")

    experts = jnp.arange(count, dtype=jnp.int32)
    hit = routes[:, :, None] == experts
    dense = jnp.sum(jnp.where(hit, gates[:, :, None], 0.0), axis=1)
    rank = probes.shape[1]
    lanes = -(-3 * max(count, rank) // 128) * 128

    def split_up(values):
        parts = []
        for _ in range(3):
            parts.append(lax.reduce_precision(values, 8, 7))
            values = values - parts[-1]
        parts = jnp.concatenate(parts, axis=1).astype(BF16)
        return jnp.pad(parts, ((0, 0), (0, lanes - parts.shape[1])))

    parts = jnp.concatenate([split_up(dense), split_up(probes)], axis=0)
    stacked = jnp.concatenate([jnp.concatenate([tokens, tangent], axis=0), parts], axis=1)
    mine = jnp.full((1,), me, jnp.int32)
    weights = (w_g, w_u, w_d)

    def up(s, pieces):
        keep, send, u, v, spread = up_call(pieces, mine, count, *weights)
        return keep, send, (u, v, spread)

    turns = {s + 1 if s else depth + 1: s for s in range(depth)}
    combined, saved, _ = phase(stacked, rows, up, turns, None, ring, across, pair, depth)

    share = width // count
    held = {"sum": jnp.zeros((rank, width), F32)}

    def down(s, pieces):
        keep, send, term = down_call(pieces, *saved[s], held["sum"], *weights)
        return keep, send, term

    def side(turn, terms):
        if turn == depth + 1:
            term = arrange_call(held["sum"], mine, count)
            held["sum"] = term[:2] + swap(term[2:], pair)
        elif turn == depth + 2:
            held["sum"] = held["sum"][0] + swap(held["sum"][1], across)
        elif turn == depth + 3:
            term = held["sum"]
            total = term[0]
            for s in range(1, depth):
                back = [(i, (i - 4 * s) % count) for i in range(count)]
                total = total + swap(term[s], back)
            held["sum"] = total
        elif turn <= depth:
            return ()
        return held["sum"]

    def settle(turn, values):
        held["sum"] = values

    turns = {s + 1: s for s in range(depth)}
    curvature_rows, _, sketch = phase(combined, None, down, turns, (side, settle), ring, across, pair, depth)
    return (curvature_rows, sketch)


def solution(mesh):
    return jax.shard_map(
        body,
        mesh=mesh,
        in_specs=(
            P(("group", "expert"), None),
            P(("group", "expert"), None),
            P(("group", "expert"), None),
            P(("group", "expert"), None),
            P(("group", "expert"), None),
            P("expert", None, None),
            P("expert", None, None),
            P("expert", None, None),
        ),
        out_specs=(P(("group", "expert"), None), P("group", "expert")),
        check_vma=False,
    )
```

```python
import functools

import jax
import jax.numpy as jnp
from jax import lax
from jax.experimental import pallas as pl
from jax.experimental.pallas import tpu as pltpu
from jax.sharding import PartitionSpec as P

BF16 = jnp.bfloat16
F32 = jnp.float32
PACK_BYTES = 56 * 1024 * 1024
UP_BYTES = 12 * 1024 * 1024
DOWN_BYTES = 12 * 1024 * 1024


def swap(values, perm):
    return lax.ppermute(values, "expert", perm)


def mm(left, right):
    return jnp.dot(left, right, preferred_element_type=F32)


def mm_t(left, right):
    return lax.dot_general(left, right, (((1,), (1,)), ((), ())), preferred_element_type=F32)


def tile_of(size, most):
    for tile in range(min(size, most), 0, -128):
        if size % tile == 0 and tile % 128 == 0:
            return tile
    return size


def load_all(copies):
    for copy in copies:
        copy.start()
    for copy in copies:
        copy.wait()


def pack_kernel(count, tokens, tangent, routes_in, gates_in, probes_in, out, whole, routes, gates, probes, sems):
    rows, width = tokens.shape
    lanes = whole.shape[1] - width
    large = [
        pltpu.make_async_copy(source, whole.at[pl.ds(j * rows, rows), pl.ds(0, width)], sems.at[j])
        for j, source in enumerate((tokens, tangent))
    ]
    small = ((routes_in, routes), (gates_in, gates), (probes_in, probes))
    early = [pltpu.make_async_copy(*both, sems.at[2 + j]) for j, both in enumerate(small)]
    for copy in early + large:
        copy.start()
    for copy in early:
        copy.wait()

    def split_up(values):
        parts = []
        for _ in range(3):
            parts.append(values.astype(BF16).astype(F32))
            values = values - parts[-1]
        parts.append(jnp.zeros((lanes - 3 * values.shape[0], rows), F32))
        return jnp.concatenate(parts, axis=0).T.astype(BF16)

    expert = lax.broadcasted_iota(jnp.int32, (count, rows), 0)
    dense = jnp.zeros((count, rows), F32)
    for k in range(routes.shape[0]):
        dense = dense + jnp.where(routes[k : k + 1, :] == expert, gates[k : k + 1, :], 0.0)
    whole[pl.ds(0, rows), pl.ds(width, lanes)] = split_up(dense)
    whole[pl.ds(rows, rows), pl.ds(width, lanes)] = split_up(probes[...])
    for copy in large:
        copy.wait()
    last = pltpu.make_async_copy(whole, out, sems.at[5])
    last.start()
    last.wait()


def pack_call(tokens, tangent, routes, gates, probes, count, lanes):
    rows, width = tokens.shape
    return pl.pallas_call(
        functools.partial(pack_kernel, count),
        in_specs=[ANY] * 5,
        out_specs=ANY,
        out_shape=jax.ShapeDtypeStruct((2 * rows, width + lanes), BF16),
        scratch_shapes=[pltpu.VMEM((2 * rows, width + lanes), BF16)]
        + [pltpu.VMEM(small.shape[::-1], small.dtype) for small in (routes, gates, probes)]
        + [pltpu.SemaphoreType.DMA((6,))],
        compiler_params=pltpu.CompilerParams(vmem_limit_bytes=PACK_BYTES),
    )(tokens, tangent, routes.T, gates.T, probes.T)


def up_kernel(f_tile, d_tile, count, *refs):
    pieces, refs = refs[:4], refs[4:]
    me, w_g, w_u, w_d, keep, send, u_out, v_out, probes_out, x_all, gates, probes, th_all, sems = refs
    width, hidden = w_g.shape
    rows = pieces[0].shape[0] // 2
    block = 4 * rows
    half = block // 2
    copies = []
    for j, piece in enumerate(pieces):
        for part in range(2):
            source = piece.at[pl.ds(part * rows, rows), pl.ds(0, width)]
            target = x_all.at[pl.ds(part * block + j * rows, rows)]
            copies.append(pltpu.make_async_copy(source, target, sems.at[4 * j + part]))
            source = piece.at[pl.ds(part * rows, rows), pl.ds(width, gates.shape[1])]
            target = (gates, probes)[part].at[pl.ds(j * rows, rows)]
            copies.append(pltpu.make_async_copy(source, target, sems.at[4 * j + 2 + part]))
    load_all(copies)
    lane = lax.broadcasted_iota(jnp.int32, gates.shape, 1) - me[0]
    hit = (lane == 0) | (lane == count) | (lane == 2 * count)
    g = jnp.sum(jnp.where(hit, gates[...].astype(F32), 0.0), axis=1, keepdims=True)
    probes_out[...] = probes[...].astype(F32).T.astype(BF16)

    def first(i, carry):
        cols = pl.ds(pl.multiple_of(i * f_tile, f_tile), f_tile)
        x = x_all[...]
        both_a = mm(x, w_g[:, cols])
        both_b = mm(x, w_u[:, cols])
        a, ta = both_a[:block], both_a[block:]
        b, tb = both_b[:block], both_b[block:]
        sig = jax.nn.sigmoid(a)
        u = (sig * (1.0 + a * (1.0 - sig))) * b * g
        v = a * sig * g
        u_out[:, cols] = u
        v_out[:, cols] = v
        th_all[:, cols] = (u * ta + v * tb).astype(BF16)
        return carry

    lax.fori_loop(0, hidden // f_tile, first, 0)

    def second(i, carry):
        cols = pl.ds(pl.multiple_of(i * d_tile, d_tile), d_tile)
        out = mm(th_all[...], w_d[:, cols]).astype(BF16)
        keep[:, cols] = out[:half]
        send[:, cols] = out[half:]
        return carry

    lax.fori_loop(0, width // d_tile, second, 0)


def down_kernel(f_tile, d_tile, rank, *refs):
    pieces, refs = refs[:4], refs[4:]
    u_in, v_in, probes, before, w_g, w_u, w_d, keep, send, term, x_all, ga, gb, sems = refs
    half = u_in.shape[0] // 2
    width, hidden = w_g.shape
    rows = pieces[0].shape[0]
    load_all(
        [
            pltpu.make_async_copy(piece, x_all.at[pl.ds(j * rows, rows)], sems.at[j])
            for j, piece in enumerate(pieces)
        ]
    )

    def first(i, carry):
        cols = pl.ds(pl.multiple_of(i * f_tile, f_tile), f_tile)
        gh = mm_t(x_all[...], w_d[cols, :])
        ga[:, cols] = (gh * u_in[:, cols]).astype(BF16)
        gb[:, cols] = (gh * v_in[:, cols]).astype(BF16)
        return carry

    lax.fori_loop(0, hidden // f_tile, first, 0)

    def second(i, carry):
        cols = pl.ds(pl.multiple_of(i * d_tile, d_tile), d_tile)
        out = (mm_t(ga[...], w_g[cols, :]) + mm_t(gb[...], w_u[cols, :])).astype(BF16)
        keep[:, cols] = out[:half]
        send[:, cols] = out[half:]
        parts = mm(probes[...], out)
        term[:, cols] = before[:, cols] + (parts[:rank] + parts[rank : 2 * rank] + parts[2 * rank : 3 * rank])
        return carry

    lax.fori_loop(0, width // d_tile, second, 0)


ANY = pl.BlockSpec(memory_space=pl.ANY)
WHOLE = pl.BlockSpec(memory_space=pltpu.VMEM)


def up_call(pieces, me, count, w_g, w_u, w_d):
    width, hidden = w_g.shape
    block, lanes = 2 * pieces[0].shape[0], pieces[0].shape[1] - width
    return pl.pallas_call(
        functools.partial(up_kernel, tile_of(hidden, 512), tile_of(width, 1792), count),
        in_specs=[ANY] * 4 + [pl.BlockSpec(memory_space=pltpu.SMEM)] + [WHOLE] * 3,
        out_specs=[WHOLE] * 5,
        out_shape=[jax.ShapeDtypeStruct((block // 2, width), BF16)] * 2
        + [jax.ShapeDtypeStruct((block, hidden), F32)] * 2
        + [jax.ShapeDtypeStruct((lanes, block), BF16)],
        scratch_shapes=[
            pltpu.VMEM((2 * block, width), BF16),
            pltpu.VMEM((block, lanes), BF16),
            pltpu.VMEM((block, lanes), BF16),
            pltpu.VMEM((block, hidden), BF16),
            pltpu.SemaphoreType.DMA((16,)),
        ],
        compiler_params=pltpu.CompilerParams(vmem_limit_bytes=UP_BYTES),
        cost_estimate=pl.CostEstimate(flops=10 * width * hidden * block, bytes_accessed=2**20, transcendentals=0),
    )(*pieces, me, w_g, w_u, w_d)


def down_call(pieces, u, v, probes, before, w_g, w_u, w_d):
    width, hidden = w_g.shape
    rank = before.shape[0]
    block = u.shape[0]
    return pl.pallas_call(
        functools.partial(down_kernel, tile_of(hidden, 512), tile_of(width, 1792), rank),
        in_specs=[ANY] * 4 + [WHOLE] * 7,
        out_specs=[WHOLE] * 3,
        out_shape=[jax.ShapeDtypeStruct((block // 2, width), BF16)] * 2 + [jax.ShapeDtypeStruct((rank, width), F32)],
        scratch_shapes=[
            pltpu.VMEM((block, width), BF16),
            pltpu.VMEM((block, hidden), BF16),
            pltpu.VMEM((block, hidden), BF16),
            pltpu.SemaphoreType.DMA((4,)),
        ],
        compiler_params=pltpu.CompilerParams(vmem_limit_bytes=DOWN_BYTES),
        cost_estimate=pl.CostEstimate(flops=6 * width * hidden * block, bytes_accessed=2**20, transcendentals=0),
    )(*pieces, u, v, probes, before, w_g, w_u, w_d)


def arrange_kernel(me, term, out):
    depth, share = out.shape[1], out.shape[3]
    plane, spot = me[0] // 4, me[0] % 4
    for d in range(4 * depth):
        back = lax.rem(plane + (depth - d // 4), depth)
        gap = spot ^ (d % 4)
        piece = (gap >> 1) | ((gap & 1) << 1)
        out[piece, back] = term[:, d * share : (d + 1) * share]


def arrange_call(term, me, count):
    rank, width = term.shape
    return pl.pallas_call(
        arrange_kernel,
        in_specs=[pl.BlockSpec(memory_space=pltpu.SMEM), WHOLE],
        out_specs=WHOLE,
        out_shape=jax.ShapeDtypeStruct((4, count // 4, rank, width // count), F32),
        compiler_params=pltpu.CompilerParams(vmem_limit_bytes=4 * 1024 * 1024),
    )(me, term)


def phase(own, split, lead, compute, turns, side, ring, across, pair, depth):
    near, far, near_mate = [own], [], []
    pieces, made, extras, ready = {}, {}, {}, {}
    moving = None
    for turn in range(2 * depth - lead):
        flight = {}
        if turn < depth:
            if turn < depth - 1:
                flight["near"] = swap(near[turn], ring)
                flight["far"] = swap(near[turn], across)
            elif split is None:
                flight["far"] = swap(near[turn], across)
            else:
                flight["far_low"] = swap(near[turn][:split], across)
                flight["far_high"] = swap(far[turn - 1][split:], ring)
            flight["near_mate"] = swap(near[turn], pair)
        if 0 <= turn - 1 < depth:
            back = turn - 1
            pieces[back] = (near[back], far[back], near_mate[back], swap(far[back], pair))
        if turn in turns:
            flight["made"] = compute(turns[turn], pieces.pop(turns[turn]))
        flight["pieces"] = dict(pieces)
        if turn - 1 in turns:
            keep, send = made[turns[turn - 1]]
            rows = keep.shape[0] // 2
            got = swap(send, pair)
            base = (keep[:rows].astype(F32) + got[:rows].astype(F32)).astype(BF16)
            outward = (keep[rows:].astype(F32) + got[rows:].astype(F32)).astype(BF16)
            flight["ready"] = (base, outward)
        due = turn - depth + 1 + lead
        if due >= 1:
            if due % depth in ready:
                due_base, crossing = ready.pop(due % depth)
            else:
                due_base, crossing = flight.pop("ready")
                flight["base"] = due_base
            flight["cross"] = swap(crossing, across)
            if due > 1:
                flight["moving"] = swap(moving, ring)
        if side is not None:
            flight["side"] = side[0](turn, extras)
        flight["waiting"] = dict(ready)
        names = list(flight)
        flight = dict(zip(names, lax.optimization_barrier([flight[name] for name in names])))
        if "near" in flight:
            near.append(flight["near"])
        if "far" in flight:
            far.append(flight["far"])
        if "far_low" in flight:
            far.append(jnp.concatenate([flight["far_low"], flight["far_high"]], axis=0))
        if "near_mate" in flight:
            near_mate.append(flight["near_mate"])
        pieces = flight["pieces"]
        if "made" in flight:
            made[turns[turn]] = flight["made"][:2]
            extras[turns[turn]] = flight["made"][2]
            if side is not None:
                side[1](turn, flight["made"][2])
        elif side is not None and turn > depth:
            side[1](turn, flight["side"])
        ready = flight["waiting"]
        if "ready" in flight:
            ready[turns[turn - 1]] = flight["ready"]
        if due >= 1:
            due_base = flight.get("base", due_base)
            total = due_base.astype(F32) + flight["cross"].astype(F32)
            if "moving" in flight:
                total = total + flight["moving"].astype(F32)
            moving = total.astype(BF16)
    return moving, extras, flight.get("side")


def body(tokens, tangent, routes, gates, probes, w_gate, w_up, w_down):
    rows, width = tokens.shape
    count = lax.axis_size("expert")
    depth = count // 4
    ring = [(i, (i + 4) % count) for i in range(count)]
    across = [(i, i ^ 2) for i in range(count)]
    pair = [(i, i ^ 1) for i in range(count)]
    w_g, w_u, w_d = w_gate[0], w_up[0], w_down[0]
    me = lax.axis_index("expert")

    rank = probes.shape[1]
    lanes = -(-3 * max(count, rank) // 128) * 128
    stacked = pack_call(tokens, tangent, routes, gates, probes, count, lanes)
    mine = jnp.full((1,), me, jnp.int32)
    weights = (w_g, w_u, w_d)

    def up(s, pieces):
        keep, send, u, v, spread = up_call(pieces, mine, count, *weights)
        return keep, send, (u, v, spread)

    turns = {s + 1: s for s in range(depth)}
    combined, saved, _ = phase(stacked, rows * 2 // 3, 1, up, turns, None, ring, across, pair, depth)

    share = width // count
    held = {"sum": jnp.zeros((rank, width), F32)}

    def down(s, pieces):
        keep, send, term = down_call(pieces, *saved[s], held["sum"], *weights)
        return keep, send, term

    def side(turn, terms):
        if turn == depth + 1:
            term = arrange_call(held["sum"], mine, count)
            held["sum"] = term[:2] + swap(term[2:], pair)
        elif turn == depth + 2:
            held["sum"] = held["sum"][0] + swap(held["sum"][1], across)
        elif turn == depth + 3:
            term = held["sum"]
            total = term[0]
            for s in range(1, depth):
                back = [(i, (i - 4 * s) % count) for i in range(count)]
                total = total + swap(term[s], back)
            held["sum"] = total
        elif turn <= depth:
            return ()
        return held["sum"]

    def settle(turn, values):
        held["sum"] = values

    turns = {s + 1: s for s in range(depth)}
    curvature_rows, _, sketch = phase(combined, None, 0, down, turns, (side, settle), ring, across, pair, depth)
    return (curvature_rows, sketch)


def solution(mesh):
    return jax.shard_map(
        body,
        mesh=mesh,
        in_specs=(
            P(("group", "expert"), None),
            P(("group", "expert"), None),
            P(("group", "expert"), None),
            P(("group", "expert"), None),
            P(("group", "expert"), None),
            P("expert", None, None),
            P("expert", None, None),
            P("expert", None, None),
        ),
        out_specs=(P(("group", "expert"), None), P("group", "expert")),
        check_vma=False,
    )
```

```python
import functools

import jax
import jax.numpy as jnp
from jax import lax
from jax.experimental import pallas as pl
from jax.experimental.pallas import tpu as pltpu
from jax.sharding import PartitionSpec as P

BF16 = jnp.bfloat16
F32 = jnp.float32
PACK_BYTES = 56 * 1024 * 1024
UP_BYTES = 12 * 1024 * 1024
DOWN_BYTES = 12 * 1024 * 1024


def swap(values, perm):
    return lax.ppermute(values, "expert", perm)


def mm(left, right):
    return jnp.dot(left, right, preferred_element_type=F32)


def mm_t(left, right):
    return lax.dot_general(left, right, (((1,), (1,)), ((), ())), preferred_element_type=F32)


def tile_of(size, most):
    for tile in range(min(size, most), 0, -128):
        if size % tile == 0 and tile % 128 == 0:
            return tile
    return size


def load_all(copies):
    for copy in copies:
        copy.start()
    for copy in copies:
        copy.wait()


def pack_kernel(count, tokens, tangent, routes_in, gates_in, probes_in, out, whole, routes, gates, probes, sems):
    rows, width = tokens.shape
    lanes = whole.shape[1] - width
    large = [
        pltpu.make_async_copy(source, whole.at[pl.ds(j * rows, rows), pl.ds(0, width)], sems.at[j])
        for j, source in enumerate((tokens, tangent))
    ]
    small = ((routes_in, routes), (gates_in, gates), (probes_in, probes))
    early = [pltpu.make_async_copy(*both, sems.at[2 + j]) for j, both in enumerate(small)]
    for copy in early + large:
        copy.start()
    for copy in early:
        copy.wait()

    def split_up(values):
        parts = []
        for _ in range(3):
            parts.append(values.astype(BF16).astype(F32))
            values = values - parts[-1]
        parts.append(jnp.zeros((lanes - 3 * values.shape[0], rows), F32))
        return jnp.concatenate(parts, axis=0).T.astype(BF16)

    expert = lax.broadcasted_iota(jnp.int32, (count, rows), 0)
    dense = jnp.zeros((count, rows), F32)
    for k in range(routes.shape[0]):
        dense = dense + jnp.where(routes[k : k + 1, :] == expert, gates[k : k + 1, :], 0.0)
    whole[pl.ds(0, rows), pl.ds(width, lanes)] = split_up(dense)
    whole[pl.ds(rows, rows), pl.ds(width, lanes)] = split_up(probes[...])
    for copy in large:
        copy.wait()
    last = pltpu.make_async_copy(whole, out, sems.at[5])
    last.start()
    last.wait()


def pack_call(tokens, tangent, routes, gates, probes, count, lanes):
    rows, width = tokens.shape
    return pl.pallas_call(
        functools.partial(pack_kernel, count),
        in_specs=[ANY] * 5,
        out_specs=ANY,
        out_shape=jax.ShapeDtypeStruct((2 * rows, width + lanes), BF16),
        scratch_shapes=[pltpu.VMEM((2 * rows, width + lanes), BF16)]
        + [pltpu.VMEM(small.shape[::-1], small.dtype) for small in (routes, gates, probes)]
        + [pltpu.SemaphoreType.DMA((6,))],
        compiler_params=pltpu.CompilerParams(vmem_limit_bytes=PACK_BYTES),
    )(tokens, tangent, routes.T, gates.T, probes.T)


def up_kernel(f_tile, d_tile, count, *refs):
    pieces, refs = refs[:4], refs[4:]
    me, w_g, w_u, w_d, keep, send, u_out, v_out, probes_out, x_all, gates, probes, th_all, sems = refs
    width, hidden = w_g.shape
    rows = pieces[0].shape[0] // 2
    block = 4 * rows
    half = block // 2
    copies = []
    for j, piece in enumerate(pieces):
        for part in range(2):
            source = piece.at[pl.ds(part * rows, rows), pl.ds(0, width)]
            target = x_all.at[pl.ds(part * block + j * rows, rows)]
            copies.append(pltpu.make_async_copy(source, target, sems.at[4 * j + part]))
            source = piece.at[pl.ds(part * rows, rows), pl.ds(width, gates.shape[1])]
            target = (gates, probes)[part].at[pl.ds(j * rows, rows)]
            copies.append(pltpu.make_async_copy(source, target, sems.at[4 * j + 2 + part]))
    load_all(copies)
    lane = lax.broadcasted_iota(jnp.int32, gates.shape, 1) - me[0]
    hit = (lane == 0) | (lane == count) | (lane == 2 * count)
    g = jnp.sum(jnp.where(hit, gates[...].astype(F32), 0.0), axis=1, keepdims=True)
    probes_out[...] = probes[...].astype(F32).T.astype(BF16)

    def first(i, carry):
        cols = pl.ds(pl.multiple_of(i * f_tile, f_tile), f_tile)
        x = x_all[...]
        both_a = mm(x, w_g[:, cols])
        both_b = mm(x, w_u[:, cols])
        a, ta = both_a[:block], both_a[block:]
        b, tb = both_b[:block], both_b[block:]
        sig = jax.nn.sigmoid(a)
        u = (sig * (1.0 + a * (1.0 - sig))) * b * g
        v = a * sig * g
        u_out[:, cols] = u
        v_out[:, cols] = v
        th_all[:, cols] = (u * ta + v * tb).astype(BF16)
        return carry

    lax.fori_loop(0, hidden // f_tile, first, 0)

    def second(i, carry):
        cols = pl.ds(pl.multiple_of(i * d_tile, d_tile), d_tile)
        out = mm(th_all[...], w_d[:, cols]).astype(BF16)
        keep[:, cols] = out[:half]
        send[:, cols] = out[half:]
        return carry

    lax.fori_loop(0, width // d_tile, second, 0)


def down_kernel(f_tile, d_tile, rank, *refs):
    pieces, refs = refs[:4], refs[4:]
    u_in, v_in, probes, before, w_g, w_u, w_d, keep, send, term, x_all, ga, gb, sems = refs
    half = u_in.shape[0] // 2
    width, hidden = w_g.shape
    rows = pieces[0].shape[0]
    load_all(
        [
            pltpu.make_async_copy(piece, x_all.at[pl.ds(j * rows, rows)], sems.at[j])
            for j, piece in enumerate(pieces)
        ]
    )

    def first(i, carry):
        cols = pl.ds(pl.multiple_of(i * f_tile, f_tile), f_tile)
        gh = mm_t(x_all[...], w_d[cols, :])
        ga[:, cols] = (gh * u_in[:, cols]).astype(BF16)
        gb[:, cols] = (gh * v_in[:, cols]).astype(BF16)
        return carry

    lax.fori_loop(0, hidden // f_tile, first, 0)

    def second(i, carry):
        cols = pl.ds(pl.multiple_of(i * d_tile, d_tile), d_tile)
        out = (mm_t(ga[...], w_g[cols, :]) + mm_t(gb[...], w_u[cols, :])).astype(BF16)
        keep[:, cols] = out[:half]
        send[:, cols] = out[half:]
        parts = mm(probes[...], out)
        term[:, cols] = before[:, cols] + (parts[:rank] + parts[rank : 2 * rank] + parts[2 * rank : 3 * rank])
        return carry

    lax.fori_loop(0, width // d_tile, second, 0)


ANY = pl.BlockSpec(memory_space=pl.ANY)
WHOLE = pl.BlockSpec(memory_space=pltpu.VMEM)


def up_call(pieces, me, count, w_g, w_u, w_d):
    width, hidden = w_g.shape
    block, lanes = 2 * pieces[0].shape[0], pieces[0].shape[1] - width
    return pl.pallas_call(
        functools.partial(up_kernel, tile_of(hidden, 512), tile_of(width, 1792), count),
        in_specs=[ANY] * 4 + [pl.BlockSpec(memory_space=pltpu.SMEM)] + [WHOLE] * 3,
        out_specs=[WHOLE] * 5,
        out_shape=[jax.ShapeDtypeStruct((block // 2, width), BF16)] * 2
        + [jax.ShapeDtypeStruct((block, hidden), F32)] * 2
        + [jax.ShapeDtypeStruct((lanes, block), BF16)],
        scratch_shapes=[
            pltpu.VMEM((2 * block, width), BF16),
            pltpu.VMEM((block, lanes), BF16),
            pltpu.VMEM((block, lanes), BF16),
            pltpu.VMEM((block, hidden), BF16),
            pltpu.SemaphoreType.DMA((16,)),
        ],
        compiler_params=pltpu.CompilerParams(vmem_limit_bytes=UP_BYTES),
        cost_estimate=pl.CostEstimate(flops=10 * width * hidden * block, bytes_accessed=2**20, transcendentals=0),
    )(*pieces, me, w_g, w_u, w_d)


def down_call(pieces, u, v, probes, before, w_g, w_u, w_d):
    width, hidden = w_g.shape
    rank = before.shape[0]
    block = u.shape[0]
    return pl.pallas_call(
        functools.partial(down_kernel, tile_of(hidden, 512), tile_of(width, 1792), rank),
        in_specs=[ANY] * 4 + [WHOLE] * 7,
        out_specs=[WHOLE] * 3,
        out_shape=[jax.ShapeDtypeStruct((block // 2, width), BF16)] * 2 + [jax.ShapeDtypeStruct((rank, width), F32)],
        scratch_shapes=[
            pltpu.VMEM((block, width), BF16),
            pltpu.VMEM((block, hidden), BF16),
            pltpu.VMEM((block, hidden), BF16),
            pltpu.SemaphoreType.DMA((4,)),
        ],
        compiler_params=pltpu.CompilerParams(vmem_limit_bytes=DOWN_BYTES),
        cost_estimate=pl.CostEstimate(flops=6 * width * hidden * block, bytes_accessed=2**20, transcendentals=0),
    )(*pieces, u, v, probes, before, w_g, w_u, w_d)


def arrange_kernel(me, term, out):
    depth, share = out.shape[1], out.shape[3]
    plane, spot = me[0] // 4, me[0] % 4
    for d in range(4 * depth):
        back = lax.rem(plane + (depth - d // 4), depth)
        gap = spot ^ (d % 4)
        piece = (gap >> 1) | ((gap & 1) << 1)
        out[piece, back] = term[:, d * share : (d + 1) * share]


def arrange_call(term, me, count):
    rank, width = term.shape
    return pl.pallas_call(
        arrange_kernel,
        in_specs=[pl.BlockSpec(memory_space=pltpu.SMEM), WHOLE],
        out_specs=WHOLE,
        out_shape=jax.ShapeDtypeStruct((4, count // 4, rank, width // count), F32),
        compiler_params=pltpu.CompilerParams(vmem_limit_bytes=4 * 1024 * 1024),
    )(me, term)


def phase(own, split, lead, compute, turns, side, ring, across, pair, depth):
    near, far, near_mate = [own], [], []
    pieces, made, extras, ready = {}, {}, {}, {}
    moving = None
    for turn in range(2 * depth - lead):
        flight = {}
        if turn < depth:
            if turn < depth - 1:
                flight["near"] = swap(near[turn], ring)
                flight["far"] = swap(near[turn], across)
            elif split == 0:
                flight["far"] = swap(far[turn - 1], ring)
            else:
                flight["far_low"] = swap(near[turn][:split], across)
                flight["far_high"] = swap(far[turn - 1][split:], ring)
            flight["near_mate"] = swap(near[turn], pair)
        if 0 <= turn - 1 < depth:
            back = turn - 1
            pieces[back] = (near[back], far[back], near_mate[back], swap(far[back], pair))
        if turn in turns:
            flight["made"] = compute(turns[turn], pieces.pop(turns[turn]))
        flight["pieces"] = dict(pieces)
        if turn - 1 in turns:
            keep, send = made[turns[turn - 1]]
            rows = keep.shape[0] // 2
            got = swap(send, pair)
            base = (keep[:rows].astype(F32) + got[:rows].astype(F32)).astype(BF16)
            outward = (keep[rows:].astype(F32) + got[rows:].astype(F32)).astype(BF16)
            flight["ready"] = (base, outward)
        due = turn - depth + 1 + lead
        if due >= 1:
            if due % depth in ready:
                due_base, crossing = ready.pop(due % depth)
            else:
                due_base, crossing = flight.pop("ready")
                flight["base"] = due_base
            flight["cross"] = swap(crossing, across)
            if due > 1:
                flight["moving"] = swap(moving, ring)
        if side is not None:
            flight["side"] = side[0](turn, extras)
        flight["waiting"] = dict(ready)
        names = list(flight)
        flight = dict(zip(names, lax.optimization_barrier([flight[name] for name in names])))
        if "near" in flight:
            near.append(flight["near"])
        if "far" in flight:
            far.append(flight["far"])
        if "far_low" in flight:
            far.append(jnp.concatenate([flight["far_low"], flight["far_high"]], axis=0))
        if "near_mate" in flight:
            near_mate.append(flight["near_mate"])
        pieces = flight["pieces"]
        if "made" in flight:
            made[turns[turn]] = flight["made"][:2]
            extras[turns[turn]] = flight["made"][2]
            if side is not None:
                side[1](turn, flight["made"][2])
        elif side is not None and turn > depth:
            side[1](turn, flight["side"])
        ready = flight["waiting"]
        if "ready" in flight:
            ready[turns[turn - 1]] = flight["ready"]
        if due >= 1:
            due_base = flight.get("base", due_base)
            total = due_base.astype(F32) + flight["cross"].astype(F32)
            if "moving" in flight:
                total = total + flight["moving"].astype(F32)
            moving = total.astype(BF16)
    return moving, extras, flight.get("side")


def body(tokens, tangent, routes, gates, probes, w_gate, w_up, w_down):
    rows, width = tokens.shape
    count = lax.axis_size("expert")
    depth = count // 4
    ring = [(i, (i + 4) % count) for i in range(count)]
    across = [(i, i ^ 2) for i in range(count)]
    pair = [(i, i ^ 1) for i in range(count)]
    w_g, w_u, w_d = w_gate[0], w_up[0], w_down[0]
    me = lax.axis_index("expert")

    rank = probes.shape[1]
    lanes = -(-3 * max(count, rank) // 128) * 128
    stacked = pack_call(tokens, tangent, routes, gates, probes, count, lanes)
    mine = jnp.full((1,), me, jnp.int32)
    weights = (w_g, w_u, w_d)

    def up(s, pieces):
        keep, send, u, v, spread = up_call(pieces, mine, count, *weights)
        return keep, send, (u, v, spread)

    turns = {s + 1: s for s in range(depth)}
    combined, saved, _ = phase(stacked, rows * 2 // 3, 1, up, turns, None, ring, across, pair, depth)

    share = width // count
    held = {"sum": jnp.zeros((rank, width), F32)}

    def down(s, pieces):
        keep, send, term = down_call(pieces, *saved[s], held["sum"], *weights)
        return keep, send, term

    def side(turn, terms):
        if turn == depth + 1:
            term = arrange_call(held["sum"], mine, count)
            term = term[:2] + swap(term[2:], pair)
            held["sum"] = term[0] + swap(term[1], across)
        elif turn == depth + 2:
            term = held["sum"]
            total = term[0]
            for s in range(1, depth):
                back = [(i, (i - 4 * s) % count) for i in range(count)]
                total = total + swap(term[s], back)
            held["sum"] = total
        elif turn <= depth:
            return ()
        return held["sum"]

    def settle(turn, values):
        held["sum"] = values

    turns = {s + 1: s for s in range(depth)}
    curvature_rows, _, sketch = phase(combined, 0, 1, down, turns, (side, settle), ring, across, pair, depth)
    return (curvature_rows, sketch)


def solution(mesh):
    return jax.shard_map(
        body,
        mesh=mesh,
        in_specs=(
            P(("group", "expert"), None),
            P(("group", "expert"), None),
            P(("group", "expert"), None),
            P(("group", "expert"), None),
            P(("group", "expert"), None),
            P("expert", None, None),
            P("expert", None, None),
            P("expert", None, None),
        ),
        out_specs=(P(("group", "expert"), None), P("group", "expert")),
        check_vma=False,
    )
```
